32 devices in a mesh: dp: 4 (over z), tensor: 8 (over y, x, core).
Axes of the slice: x: 2, y: 2, z: 4, core: 2. Of those that a mesh axis runs over, the one named last changes fastest.
Arguments:
- pages: bfloat16 [2, 16, 64, 2048], P(None, 'dp', None, 'tensor'), may hold values from -8 to 8
- page_table: int32 [4, 2], replicated, may hold values from 0 to 15, as said below
- page_count: int32 [4], replicated, may hold values from 1 to 2
- last_len: int32 [4], replicated, may hold values from 1 to 64
- targets: int32 [4, 128], P('dp'), may hold values from 0 to 65535
- mix_key: float32 [2, 2048], P(None, 'tensor'), may hold values from 0.05 to 0.95
- w_key: bfloat16 [2, 2048, 8192], P(None, None, 'tensor'), may hold values from -0.125 to 0.125
- w_value: bfloat16 [2, 8192, 2048], P(None, 'tensor'), may hold values from -0.0625 to 0.0625
- ln_gain: float32 [2, 2048], replicated, may hold values from 0.5 to 1.5
- ln_bias: float32 [2, 2048], replicated, may hold values from -2 to 2
- head: bfloat16 [2, 2048, 65536], P(None, 'dp', 'tensor'), may hold values from -8 to 8
Outputs:
- token_logprob: float32 [4, 128], P('dp', 'tensor')
- ratio_sum: float32 [4], P('dp')
The draws below stay inside these ranges and needn't reach their ends.
Inputs may be any that keep to these rules, and one draw needn't show every extreme that they name: Entries are distinct; the page lives on dp device page_table[r, p] // 4.
All inputs are finite; a program needn't handle non-finite values.
Results may differ from the reference program's by a relative error of at most 0.0029.
The reference program's roundings to bfloat16 on the way (of `states`, `shifted`, `key_act` and `normed`) count: a program that leaves them out, or rounds other values in their place, can miss the bound.
Values may be sent and summed in bfloat16 or wider, within the bound.
No kernel may reach another device: no remote copies, remote signals or barrier semaphores. Data moves between devices by JAX's collectives and lax.ppermute only.
A program may use at most 192 MiB of HBM per device.

```python
import math
import jax
import jax.numpy as jnp
from jax import lax

D = 2048
FF = 8192
VOCAB = 65536
PAGE = 64
MAXP = 2
ROLLS = 4
NPAGES = 16
SLOTS = 128


def signs_of(key):
    flips = jax.random.bernoulli(jax.random.fold_in(key, 101), 0.5, (D,))
    return jnp.where(flips, 1.0, -1.0).astype(jnp.float32)


def draw_pages(key, part):
    array_shape = (2, NPAGES, PAGE, D)
    feature = 0.6 * jnp.exp(jnp.log(3.0) * jnp.arange(D, dtype=jnp.float32) / D)
    values = jnp.clip(jax.random.normal(jax.random.fold_in(key, 1), array_shape, jnp.float32), -4.0, 4.0) * feature
    amplitude = jax.random.uniform(jax.random.fold_in(key, 2), (2, NPAGES, 1, 1), jnp.float32, 0.8, 1.2)
    leading = (jnp.arange(PAGE) < 2)[None, None, :, None]
    values = jnp.where(leading, signs_of(key)[None, None, None, :] * amplitude, values)
    return values.astype(jnp.bfloat16)


def draw_head(key, part):
    array_shape = (2, D, VOCAB)
    spread = 3.0 / math.sqrt(D)
    base_draw = jnp.clip(jax.random.normal(jax.random.fold_in(key, 4), array_shape, jnp.float32), -4.0, 4.0) * spread
    first_col = jax.random.randint(jax.random.fold_in(key, 5), (), 0, VOCAB - 1)
    column = jnp.arange(VOCAB)[None, None, :]
    aligned = signs_of(key)[None, :, None] * (400.0 / D)
    base_draw = jnp.where(column == first_col, aligned, jnp.where(column == first_col + 1, aligned * 1.006, base_draw))
    return base_draw.astype(jnp.bfloat16)


def draw_page_table(key, part):
    middle = 1 + jax.random.permutation(jax.random.fold_in(key, 7), NPAGES - 2)
    chosen_rows = jnp.concatenate([jnp.array([0, NPAGES - 1], jnp.int32), middle[:ROLLS * MAXP - 2].astype(jnp.int32)])
    shuffled = jax.random.permutation(jax.random.fold_in(key, 17), chosen_rows)
    return shuffled.reshape(ROLLS, MAXP).astype(jnp.int32)


def draw_page_count(key, part):
    first_draw = jax.random.randint(jax.random.fold_in(key, 8), (ROLLS,), 0, MAXP)
    second_draw = jax.random.randint(jax.random.fold_in(key, 9), (ROLLS,), 0, MAXP)
    counts = 1 + first_draw * second_draw // (MAXP - 1)
    chosen = jax.random.randint(jax.random.fold_in(key, 10), (), 0, ROLLS)
    return jnp.where(jnp.arange(ROLLS) == chosen, MAXP, counts).astype(jnp.int32)


def draw_last_len(key, part):
    lengths = jax.random.randint(jax.random.fold_in(key, 12), (ROLLS,), 1, PAGE + 1)
    chosen = jax.random.randint(jax.random.fold_in(key, 13), (), 0, ROLLS)
    return jnp.where(jnp.arange(ROLLS) == chosen, PAGE, lengths).astype(jnp.int32)


def plant(values, own_key, low, high):
    dims = values.shape
    place = [jax.random.randint(jax.random.fold_in(own_key, axis), (), 0, dims[axis]) for axis in range(len(dims))]
    values = values.at[tuple(place)].set(low)
    longest = dims.index(max(dims))
    place[longest] = (place[longest] + 1) % dims[longest]
    return values.at[tuple(place)].set(high)


def level_of(own_key, dims, split, smallest, top_value):
    gain = 1.0
    for position, parts in split:
        heights = jax.random.uniform(jax.random.fold_in(jax.random.fold_in(own_key, 6), position), (parts,), jnp.float32, smallest / len(split), top_value / len(split))
        gain = gain * jnp.repeat(jnp.exp(heights), dims[position] // parts).reshape((-1,) + (1,) * (len(dims) - 1 - position))
    return gain


def bell_draw(key, dims, width, limit, cuts=(), kind=jnp.bfloat16):
    values = jax.random.normal(key, dims, jnp.float32) * width
    if len(cuts) > 0:
        values = level_of(key, dims, cuts, -0.22, 0.18) * values
    return jnp.clip(values, min=-limit, max=limit).astype(kind)


def setup_inputs(seed: int = 0) -> dict:
    keys = jax.random.split(jax.random.key(seed), 12)
    return {
        "pages": draw_pages(jax.random.fold_in(keys[11], 71), 0),
        "page_table": draw_page_table(jax.random.fold_in(keys[11], 71), 0),
        "page_count": draw_page_count(jax.random.fold_in(keys[11], 71), 0),
        "last_len": draw_last_len(jax.random.fold_in(keys[11], 71), 0),
        "targets": plant(jax.random.randint(keys[4], (ROLLS, SLOTS), 0, VOCAB), jax.random.fold_in(keys[4], 1), 0, VOCAB - 1).astype(jnp.int32),
        "mix_key": jnp.clip(0.05 + 0.9 * jax.random.uniform(keys[5], (2, D), jnp.float32) ** level_of(keys[5], (2, D), ((1, 8),), -0.2, 0.2), 0.05, 0.95),
        "w_key": bell_draw(keys[6], (2, D, FF), D ** -0.5, 0.125, ((2, 8),)),
        "w_value": bell_draw(keys[7], (2, FF, D), FF ** -0.5, 0.0625, ((1, 8),)),
        "ln_gain": jnp.clip(1.0 + 0.1 * jax.random.normal(keys[8], (2, D), jnp.float32), 0.5, 1.5),
        "ln_bias": bell_draw(keys[9], (2, D), 0.3, 2.0, (), jnp.float32),
        "head": draw_head(jax.random.fold_in(keys[11], 71), 0),
    }


epsilon = 1e-05

def reference(pages, page_table, page_count, last_len, targets, mix_key, w_key, w_value, ln_gain, ln_bias, head):
    picked = pages[:, page_table]
    live = jnp.arange(MAXP)[None, :] < page_count[:, None]
    picked = jnp.where(live[None, :, :, None, None], picked, jnp.zeros_like(picked))
    states = jnp.transpose(picked.reshape(2, ROLLS, MAXP * PAGE, D), (1, 0, 2, 3))
    lengths = (page_count - 1) * PAGE + last_len
    key_full = w_key.astype(jnp.float32)
    value_full = w_value.astype(jnp.float32)
    head_full = head.astype(jnp.float32)

    def one_rollout(inputs):
        state, target_row, length = inputs
        state_f = state.astype(jnp.float32)
        previous = jnp.concatenate([jnp.zeros((2, 1, D), jnp.float32), state_f[:, :-1]], axis=1)
        shifted = (state_f + (previous - state_f) * mix_key[:, None, :]).astype(jnp.bfloat16)
        hidden = jnp.einsum('msd,mdf->msf', shifted.astype(jnp.float32), key_full)
        key_act = (jnp.maximum(hidden, 0.0) ** 2).astype(jnp.bfloat16)
        residual = state_f + jnp.einsum('msf,mfd->msd', key_act.astype(jnp.float32), value_full)
        average = lax.optimization_barrier(jnp.sum(residual, axis=-1)) / D
        variance = lax.optimization_barrier(jnp.sum(residual * residual, axis=-1)) / D - average * average
        normed = ((residual - average[..., None]) * lax.rsqrt(variance + epsilon)[..., None] * ln_gain[:, None, :] + ln_bias[:, None, :]).astype(jnp.bfloat16)
        logits = jnp.einsum('msd,mdv->msv', normed.astype(jnp.float32), head_full)
        peak = lax.optimization_barrier(jnp.max(logits, axis=-1))
        totals = lax.optimization_barrier(jnp.sum(jnp.exp(logits - peak[..., None]), axis=-1))
        target_logit = jnp.take_along_axis(logits, jnp.broadcast_to(target_row[None, :, None], (2, MAXP * PAGE, 1)), axis=2)[..., 0]
        logp = target_logit - peak - jnp.log(totals)
        valid = jnp.arange(MAXP * PAGE) < length
        token_row = jnp.where(valid, logp[0], 0.0)
        ratio = jnp.sum(jnp.where(valid, logp[0] - logp[1], 0.0))
        return (token_row, ratio)
    token_logprob, ratio_sum = lax.map(one_rollout, (states, targets, lengths))
    return (token_logprob, ratio_sum)
```

```python
import jax
import jax.numpy as jnp
from jax import lax
from jax.sharding import PartitionSpec as P

epsilon = 1e-05


def swap(value, axis, mask):
    count = lax.axis_size(axis)
    return lax.ppermute(value, axis, [(i, i ^ mask) for i in range(count)])


def ordered(pieces, index):
    pieces = list(pieces)
    bit = 1
    while bit < len(pieces):
        flip = (index & bit) != 0
        pieces = [jnp.where(flip, pieces[k ^ bit], pieces[k]) for k in range(len(pieces))]
        bit *= 2
    return pieces


def gather_chips(value):
    count = lax.axis_size("tensor")
    far = [value] + [swap(value, "tensor", k) for k in range(2, count, 2)]
    pieces = []
    for piece in far:
        pieces += [piece, swap(piece, "tensor", 1)]
    return pieces


def spread(value, axis):
    return [value] + [swap(value, axis, k) for k in range(1, lax.axis_size(axis))]


def body(
    pages,
    page_table,
    page_count,
    last_len,
    targets,
    mix_key,
    w_key,
    w_value,
    ln_gain,
    ln_bias,
    head,
):
    tensor_count = lax.axis_size("tensor")
    layer_count = lax.axis_size("dp")
    layer = lax.axis_index("dp")
    place = lax.axis_index("tensor")
    models, rows_held, page_len, width_local = pages.shape
    width = ln_gain.shape[1]
    page_cap = page_table.shape[1]
    slot_count = page_cap * page_len
    share = slot_count // tensor_count
    depth = head.shape[1]
    vocab_held = head.shape[2]
    vocab_part = vocab_held // layer_count

    states = None
    own_rows = page_table[layer]
    for k in range(layer_count):
        wanted = page_table[layer ^ k]
        block = jnp.take(pages, wanted % rows_held, axis=1)
        got = block if k == 0 else swap(block, "dp", k)
        here = (own_rows // rows_held) == (layer ^ k)
        here = jnp.logical_and(here, jnp.arange(page_cap) < page_count[layer])
        got = jnp.where(here[None, :, None, None], got, jnp.zeros_like(got))
        states = got if states is None else states + got

    head, _ = lax.optimization_barrier((head, states))
    head_parts = []
    for k in range(layer_count):
        part = lax.dynamic_slice_in_dim(head, (layer ^ k) * vocab_part, vocab_part, 2)
        head_parts.append(part if k == 0 else swap(part, "dp", k))

    states = states.reshape(models, slot_count, width_local)
    state_f = states.astype(jnp.float32)
    previous = jnp.concatenate(
        [jnp.zeros((models, 1, width_local), jnp.float32), state_f[:, :-1]], axis=1
    )
    shifted = (state_f + (previous - state_f) * mix_key[:, None, :]).astype(jnp.bfloat16)
    shifted = jnp.concatenate(ordered(gather_chips(shifted), place), axis=2)
    hidden = jnp.einsum("msd,mdf->msf", shifted, w_key, preferred_element_type=jnp.float32)
    key_act = (jnp.maximum(hidden, 0.0) ** 2).astype(jnp.bfloat16)
    mixed = jnp.einsum("msf,mfd->msd", key_act, w_value, preferred_element_type=jnp.float32)
    mine = (jnp.arange(tensor_count) == place)[None, None, :, None]
    mixed = mixed.reshape(models, slot_count, tensor_count, width_local)
    mixed = (mixed + jnp.where(mine, state_f[:, :, None, :], 0.0)).reshape(
        models, slot_count, width
    )

    half = jnp.stack([mixed[:, k * share : (k + 1) * share] for k in range(tensor_count)])
    half = half.reshape((tensor_count // 2, 2) + half.shape[1:])
    core = place % 2
    keep = lax.dynamic_index_in_dim(half, core, 1, False)
    give = lax.dynamic_index_in_dim(half, 1 - core, 1, False)
    keep = keep + swap(give, "tensor", 1)
    chip = place // 2
    residual = lax.dynamic_index_in_dim(keep, chip, 0, False)
    for k in range(1, tensor_count // 2):
        residual = residual + swap(
            lax.dynamic_index_in_dim(keep, chip ^ k, 0, False), "tensor", 2 * k
        )

    average = jnp.sum(residual, axis=-1) / width
    variance = jnp.sum(residual * residual, axis=-1) / width - average * average
    normed = (
        (residual - average[..., None]) * lax.rsqrt(variance + epsilon)[..., None]
    ) * ln_gain[:, None, :] + ln_bias[:, None, :]
    normed = normed.astype(jnp.bfloat16)

    column = jnp.stack(ordered(spread(normed, "dp"), layer), axis=1)
    everything = jnp.stack(ordered(gather_chips(column), place), axis=2)
    everything = everything.reshape(models, layer_count * slot_count, width)

    logits = None
    for k in range(layer_count):
        features = lax.dynamic_slice_in_dim(everything, (layer ^ k) * depth, depth, 2)
        term = jnp.einsum(
            "msd,mdv->msv", features, head_parts[k], preferred_element_type=jnp.float32
        )
        logits = term if logits is None else logits + term

    wanted = jnp.concatenate(ordered(spread(targets, "dp"), layer), axis=0).reshape(-1)
    first = place * vocab_held + layer * vocab_part
    matches = (jnp.arange(vocab_part) + first)[None, None, :] == wanted[None, :, None]
    peak = jnp.max(logits, axis=-1)
    totals = jnp.sum(jnp.exp(logits - peak[..., None]), axis=-1)
    target_logit = jnp.sum(jnp.where(matches, logits, 0.0), axis=-1)
    stats = jnp.stack([peak, totals, target_logit])

    stats = stats.reshape(3, models, layer_count, slot_count)
    mine = []
    for k in range(layer_count):
        part = lax.dynamic_index_in_dim(stats, layer ^ k, 2, False)
        mine.append(part if k == 0 else swap(part, "dp", k))
    mine = jnp.concatenate(ordered(gather_chips(jnp.stack(ordered(mine, layer))), place))
    top = jnp.max(mine[:, 0], axis=0)
    totals = jnp.sum(mine[:, 1] * jnp.exp(mine[:, 0] - top), axis=0)
    logp = jnp.sum(mine[:, 2], axis=0) - top - jnp.log(totals)

    length = (page_count[layer] - 1) * page_len + last_len[layer]
    valid = jnp.arange(slot_count) < length
    policy_row = jnp.where(valid, logp[0], 0.0)
    ratio = jnp.sum(jnp.where(valid, logp[0] - logp[1], 0.0))
    token_part = lax.dynamic_slice_in_dim(policy_row, place * share, share)[None, :]
    return (token_part, ratio[None])


def solution(mesh):
    placed = (
        P(None, "dp", None, "tensor"),
        P(),
        P(),
        P(),
        P("dp", None),
        P(None, "tensor"),
        P(None, None, "tensor"),
        P(None, "tensor", None),
        P(),
        P(),
        P(None, "dp", "tensor"),
    )
    return jax.shard_map(
        body, mesh=mesh, in_specs=placed, out_specs=(P("dp", "tensor"), P("dp")), check_vma=False
    )
```

```python
import functools

import jax
import jax.numpy as jnp
from jax import lax
from jax.experimental.layout import Layout, with_layout_constraint
from jax.sharding import PartitionSpec as P

epsilon = 1e-05


def swap(value, axis, mask):
    count = lax.axis_size(axis)
    return lax.ppermute(value, axis, [(i, i ^ mask) for i in range(count)])


def ordered(pieces, index):
    pieces = list(pieces)
    bit = 1
    while bit < len(pieces):
        flip = (index & bit) != 0
        pieces = [jnp.where(flip, pieces[k ^ bit], pieces[k]) for k in range(len(pieces))]
        bit *= 2
    return pieces


def gather_chips(value):
    count = lax.axis_size("tensor")
    far = [value] + [swap(value, "tensor", k) for k in range(2, count, 2)]
    pieces = []
    for piece in far:
        pieces += [piece, swap(piece, "tensor", 1)]
    return pieces


def plain(value):
    return with_layout_constraint(value, Layout(major_to_minor=tuple(range(value.ndim))))


def spread(value, axis):
    return [value] + [swap(value, axis, k) for k in range(1, lax.axis_size(axis))]


def routes(models):
    bits = lax.axis_size("tensor").bit_length() - 1
    return [[1 + (b + m) % (bits - 1) for b in range(bits - 1)] for m in range(models)]


def gather_tensor(value, place, route):
    bits = route + [0]
    for bit in bits:
        other = swap(value, "tensor", 1 << bit)
        flip = ((place >> bit) & 1) != 0
        value = jnp.stack([jnp.where(flip, other, value), jnp.where(flip, value, other)])
    seen = bits[::-1]
    order = [seen.index(b) for b in sorted(bits, reverse=True)]
    rest = list(range(len(bits), value.ndim))
    value = value.transpose(order + rest)
    return value.reshape((1 << len(bits),) + value.shape[len(bits) :])


def scatter_tensor(value, place, route):
    count = value.shape[0]
    left = list(range(count.bit_length() - 2, -1, -1))
    value = value.reshape((2,) * len(left) + value.shape[1:])
    for bit in [0] + route:
        axis = left.index(bit)
        mine = (place >> bit) & 1
        keep = lax.dynamic_index_in_dim(value, mine, axis, False)
        give = lax.dynamic_index_in_dim(value, 1 - mine, axis, False)
        value = keep + swap(give, "tensor", 1 << bit)
        left.remove(bit)
    return value


def section(live, work, *operands):
    shapes = jax.eval_shape(work, *operands)
    idle = lambda *_: jax.tree.map(lambda s: jnp.zeros(s.shape, s.dtype), shapes)
    return lax.cond(live, work, idle, *operands)


def reduced(logits, first, wanted):
    matches = (jnp.arange(logits.shape[-1]) + first)[None, :] == wanted[:, None]
    peak = jnp.max(logits, axis=-1)
    totals = jnp.sum(jnp.exp(logits - peak[..., None]), axis=-1)
    return peak, totals, jnp.sum(jnp.where(matches, logits, 0.0), axis=-1)


def both(one, other):
    peak = jnp.maximum(one[0], other[0])
    totals = one[1] * jnp.exp(one[0] - peak) + other[1] * jnp.exp(other[0] - peak)
    return peak, totals, one[2] + other[2]


lowest = -3e38
steps = 8


def chained(rows, everything, head, targets, lengths, vocab_first, near, far, early, late, part, beside):
    layer = lax.axis_index("dp")
    models, depth = head.shape[:2]
    slot_count = everything.shape[1] // lengths.shape[0]
    outer = jnp.logical_or(layer == 0, layer == 3)
    ends = jnp.cumsum(lengths)
    starts = ends - lengths
    packed = jnp.arange(rows)
    rollout = jnp.sum(packed[:, None] >= ends[None, :], axis=1)
    offset = jnp.sum(
        jnp.where(rollout[:, None] == jnp.arange(lengths.shape[0])[None, :], starts[None, :], 0), axis=1
    )
    source = jnp.where(packed < ends[-1], rollout * slot_count + packed - offset, -1)
    picks = source[:, None] == jnp.arange(everything.shape[1])[None, :]
    wanted = jnp.sum(jnp.where(picks, targets[None, :], 0), axis=1)
    features = lax.dynamic_slice_in_dim(everything, layer * depth, depth, 2)
    features = jnp.einsum(
        "kt,mtd->mkd", picks.astype(jnp.bfloat16), features, preferred_element_type=jnp.float32
    ).astype(jnp.bfloat16)
    features = [features[m] for m in range(models)]
    width = part // steps

    def product(model, first):
        columns = lax.dynamic_slice(head, (model, 0, first), (1, depth, width))[0]
        return jnp.dot(features[model], columns, preferred_element_type=jnp.float32)

    into, out = [(0, 1), (3, 2)], [(1, 0), (2, 3)]
    side = [None] * models
    middle = [None] * models
    found = [[] for _ in range(models)]
    for s in range(-1, steps + 1):
        for m in range(models):
            if s >= 0:
                features[m], side[m], middle[m] = lax.optimization_barrier(
                    (features[m], side[m], middle[m])
                )
            first = jnp.where(outer, far + (s + 1) * width, near + (s - 1) * width)
            give = product(m, first)
            if s >= 1:
                give = give + jnp.where(outer, 0.0, middle[m])
            perm = (into if s + 1 < steps else []) + (out if s >= 1 else [])
            got = lax.ppermute(give, "dp", perm)
            if 0 <= s < steps:
                middle[m] = lax.ppermute(
                    side[m] + product(m, far + s * width), "dp", [(1, 2), (2, 1)]
                )
            side[m] = got
            if s >= 1:
                begin = near + (s - 1) * width
                found[m].append(reduced(got + product(m, begin), vocab_first + begin, wanted))
        if s == 1:
            everything, side = lax.optimization_barrier((everything, side))
            aside = jnp.stack(beside(everything, early, late))
    each = []
    for m in range(models):
        total = found[m][0]
        for more in found[m][1:]:
            total = both(total, more)
        each.append(total)
    peak, totals, target_logit = [jnp.stack(t) for t in zip(*each)]
    stats = jnp.stack(
        [
            jnp.where(outer, peak, lowest),
            jnp.where(outer, totals, 0.0),
            jnp.where(outer, target_logit, 0.0),
        ]
    )
    stats = jnp.pad(stats, ((0, 0), (0, 0), (0, slot_count)))
    stats = jnp.stack(
        [lax.dynamic_slice_in_dim(stats, starts[r], slot_count, 2) for r in range(lengths.shape[0])],
        axis=2,
    )
    return jnp.stack(both(stats, aside.reshape(stats.shape)))


def body(
    pages,
    page_table,
    page_count,
    last_len,
    targets,
    mix_key,
    w_key,
    w_value,
    ln_gain,
    ln_bias,
    head,
):
    tensor_count = lax.axis_size("tensor")
    layer_count = lax.axis_size("dp")
    layer = lax.axis_index("dp")
    place = lax.axis_index("tensor")
    models, rows_held, page_len, width_local = pages.shape
    width = ln_gain.shape[1]
    page_cap = page_table.shape[1]
    slot_count = page_cap * page_len
    share = slot_count // tensor_count
    depth = head.shape[1]
    vocab_held = head.shape[2]
    vocab_part = vocab_held // layer_count

    states = None
    own_rows = page_table[layer]
    for k in range(layer_count):
        wanted = page_table[layer ^ k]
        block = jnp.take(pages, wanted % rows_held, axis=1)
        got = block if k == 0 else swap(block, "dp", k)
        here = (own_rows // rows_held) == (layer ^ k)
        here = jnp.logical_and(here, jnp.arange(page_cap) < page_count[layer])
        got = jnp.where(here[None, :, None, None], got, jnp.zeros_like(got))
        states = got if states is None else states + got

    lengths = (page_count - 1) * page_len + last_len
    wanted = jnp.concatenate(ordered(spread(targets, "dp"), layer), axis=0).reshape(-1)
    head, states, wanted = lax.optimization_barrier((head, states, wanted))

    chain = layer_count == 4
    whole = vocab_part // 4 if chain else vocab_part

    def columns(first, count):
        parts = []
        for k in range(layer_count):
            start = (layer ^ k) * whole + first
            part = plain(lax.dynamic_slice_in_dim(head, start, count, 2))
            parts.append(part if k == 0 else plain(swap(part, "dp", k)))
        return parts

    split = whole // 2
    early = columns(0, split)
    live = page_count[0] > 0
    tracks = routes(models)

    states = states.reshape(models, slot_count, width_local)
    state_f = states.astype(jnp.float32)
    previous = jnp.concatenate(
        [jnp.zeros((models, 1, width_local), jnp.float32), state_f[:, :-1]], axis=1
    )
    shifted = (state_f + (previous - state_f) * mix_key[:, None, :]).astype(jnp.bfloat16)

    def mix(shifted, state_f):
        mine = (jnp.arange(tensor_count) == place)[None, None, :, None]
        value = jnp.stack([gather_tensor(shifted[m], place, tracks[m]) for m in range(models)])
        value = value.transpose(0, 2, 1, 3).reshape(models, slot_count, width)
        hidden = jnp.einsum("msd,mdf->msf", value, w_key, preferred_element_type=jnp.float32)
        key_act = (jnp.maximum(hidden, 0.0) ** 2).astype(jnp.bfloat16)
        mixed = jnp.einsum("msf,mfd->msd", key_act, w_value, preferred_element_type=jnp.float32)
        mixed = mixed.reshape(models, slot_count, tensor_count, width_local)
        mixed = mixed + jnp.where(mine, state_f[:, :, None, :], 0.0)
        mixed = mixed.reshape(models, tensor_count, share, width)
        rows = []
        for m in range(models):
            residual = scatter_tensor(mixed[m], place, tracks[m])
            average = jnp.sum(residual, axis=-1) / width
            variance = jnp.sum(residual * residual, axis=-1) / width - average * average
            normed = (
                (residual - average[..., None]) * lax.rsqrt(variance + epsilon)[..., None]
            ) * ln_gain[m] + ln_bias[m]
            rows.append(normed.astype(jnp.bfloat16))
        return jnp.stack(rows)

    normed = section(live, mix, shifted, state_f)
    normed, early = lax.optimization_barrier((normed, early))
    layers = jnp.stack(ordered(spread(normed, "dp"), layer), axis=1)
    layers, head = lax.optimization_barrier((layers, head))
    late = columns(split, whole - split)

    def everywhere(column):
        values = []
        for m in range(models):
            value = gather_tensor(column[m], place, tracks[m]).transpose(1, 0, 2, 3)
            values.append(value.reshape(layer_count * slot_count, width))
        return jnp.stack(values)

    everything = section(live, everywhere, layers)

    def statistics(features, parts, first):
        logits = None
        for k in range(layer_count):
            rows = lax.dynamic_slice_in_dim(features, (layer ^ k) * depth, depth, 2)
            term = jnp.einsum("msd,mdv->msv", rows, parts[k], preferred_element_type=jnp.float32)
            logits = term if logits is None else logits + term
        start = place * vocab_held + layer * whole + first
        return reduced(logits, start, wanted)

    everything, early, late = lax.optimization_barrier((everything, early, late))
    if chain:
        part = (vocab_held - layer_count * whole) // 2
        low = layer < 2
        near = layer_count * whole + jnp.where(low, 0, part)
        far = layer_count * whole + jnp.where(low, part, 0)
        sizes = [224, 256, 288, 320, 352, 384, layer_count * slot_count]
        beside = lambda value, e, l: both(statistics(value, e, 0), statistics(value, l, split))
        branches = [
            functools.partial(chained, rows, part=part, beside=beside) for rows in sizes
        ]
        bucket = sum((jnp.sum(lengths) > size).astype(jnp.int32) for size in sizes[:-1])
        stats = lax.switch(
            bucket,
            branches,
            everything,
            head,
            wanted,
            lengths,
            place * vocab_held,
            near,
            far,
            early,
            late,
        )
    else:
        stats = both(statistics(everything, early, 0), statistics(everything, late, split))
        stats = jnp.stack(stats).reshape(3, models, layer_count, slot_count)

    stats = stats.reshape(3, models, layer_count, slot_count)
    mine = []
    for k in range(layer_count):
        part = lax.dynamic_index_in_dim(stats, layer ^ k, 2, False)
        mine.append(part if k == 0 else swap(part, "dp", k))
    mine = jnp.concatenate(ordered(gather_chips(jnp.stack(ordered(mine, layer))), place))
    top = jnp.max(mine[:, 0], axis=0)
    totals = jnp.sum(mine[:, 1] * jnp.exp(mine[:, 0] - top), axis=0)
    logp = jnp.sum(mine[:, 2], axis=0) - top - jnp.log(totals)

    valid = jnp.arange(slot_count) < lengths[layer]
    policy_row = jnp.where(valid, logp[0], 0.0)
    ratio = jnp.sum(jnp.where(valid, logp[0] - logp[1], 0.0))
    token_part = lax.dynamic_slice_in_dim(policy_row, place * share, share)[None, :]
    return (token_part, ratio[None])


def solution(mesh):
    placed = (
        P(None, "dp", None, "tensor"),
        P(),
        P(),
        P(),
        P("dp", None),
        P(None, "tensor"),
        P(None, None, "tensor"),
        P(None, "tensor", None),
        P(),
        P(),
        P(None, "dp", "tensor"),
    )
    return jax.shard_map(
        body, mesh=mesh, in_specs=placed, out_specs=(P("dp", "tensor"), P("dp")), check_vma=False
    )
```

```python
import functools

import jax
import jax.numpy as jnp
from jax import lax
from jax.experimental import pallas as pl
from jax.experimental.pallas import tpu as pltpu
from jax.experimental.layout import Layout, with_layout_constraint
from jax.sharding import PartitionSpec as P

epsilon = 1e-05


def swap(value, axis, mask):
    count = lax.axis_size(axis)
    return lax.ppermute(value, axis, [(i, i ^ mask) for i in range(count)])


def ordered(pieces, index):
    pieces = list(pieces)
    bit = 1
    while bit < len(pieces):
        flip = (index & bit) != 0
        pieces = [jnp.where(flip, pieces[k ^ bit], pieces[k]) for k in range(len(pieces))]
        bit *= 2
    return pieces


def gather_chips(value):
    count = lax.axis_size("tensor")
    far = [value] + [swap(value, "tensor", k) for k in range(2, count, 2)]
    pieces = []
    for piece in far:
        pieces += [piece, swap(piece, "tensor", 1)]
    return pieces


def plain(value):
    return with_layout_constraint(value, Layout(major_to_minor=tuple(range(value.ndim))))


def spread(value, axis):
    return [value] + [swap(value, axis, k) for k in range(1, lax.axis_size(axis))]


def routes(models):
    bits = lax.axis_size("tensor").bit_length() - 1
    return [[1 + (b + m) % (bits - 1) for b in range(bits - 1)] for m in range(models)]


def gather_tensor(value, place, route):
    bits = route + [0]
    for bit in bits:
        other = swap(value, "tensor", 1 << bit)
        flip = ((place >> bit) & 1) != 0
        value = jnp.stack([jnp.where(flip, other, value), jnp.where(flip, value, other)])
    seen = bits[::-1]
    order = [seen.index(b) for b in sorted(bits, reverse=True)]
    rest = list(range(len(bits), value.ndim))
    value = value.transpose(order + rest)
    return value.reshape((1 << len(bits),) + value.shape[len(bits) :])


def scatter_tensor(value, place, route):
    count = value.shape[0]
    left = list(range(count.bit_length() - 2, -1, -1))
    value = value.reshape((2,) * len(left) + value.shape[1:])
    for bit in [0] + route:
        axis = left.index(bit)
        mine = (place >> bit) & 1
        keep = lax.dynamic_index_in_dim(value, mine, axis, False)
        give = lax.dynamic_index_in_dim(value, 1 - mine, axis, False)
        value = keep + swap(give, "tensor", 1 << bit)
        left.remove(bit)
    return value


def section(live, work, *operands):
    shapes = jax.eval_shape(work, *operands)
    idle = lambda *_: jax.tree.map(lambda s: jnp.zeros(s.shape, s.dtype), shapes)
    return lax.cond(live, work, idle, *operands)


def reduced(logits, first, wanted):
    matches = (jnp.arange(logits.shape[-1]) + first)[None, :] == wanted[:, None]
    peak = jnp.max(logits, axis=-1)
    totals = jnp.sum(jnp.exp(logits - peak[..., None]), axis=-1)
    return peak, totals, jnp.sum(jnp.where(matches, logits, 0.0), axis=-1)


def both(one, other):
    peak = jnp.maximum(one[0], other[0])
    totals = one[1] * jnp.exp(one[0] - peak) + other[1] * jnp.exp(other[0] - peak)
    return peak, totals, one[2] + other[2]


lowest = -3e38
steps = 8


lanes = 128
settings = pltpu.CompilerParams(vmem_limit_bytes=40 << 20)


def fold(logits, ids, wanted, peak, totals, target):
    top = jnp.maximum(peak, logits)
    totals = totals * jnp.exp(peak - top) + jnp.exp(logits - top)
    return top, totals, target + jnp.where(ids == wanted, logits, 0.0)


def by_rows(count, work, group=32):
    def one(i, _):
        work(pl.ds(pl.multiple_of(i * group, group), group))
        return 0

    lax.fori_loop(0, count // group, one, 0)


def step_kernel(
    at, features, far, near, side, middle, wanted, old, give, across, new, product, *, start, hear, end, last
):
    outer = at[2] != 0
    rows = features.shape[0]

    def multiply(r):
        value = features[r]
        if not end:
            give[r] = jnp.dot(value, far[0], preferred_element_type=jnp.float32)
        if start or last:
            product[r] = jnp.dot(value, near[0], preferred_element_type=jnp.float32)

    by_rows(rows, multiply, max(g for g in range(16, 113, 16) if rows % g == 0))
    if last:

        @pl.when(outer)
        def _():
            def finish(r):
                top, totals, target = old[0, r], old[1, r], old[2, r]
                for tile in range(side.shape[1] // lanes):
                    c = slice(tile * lanes, (tile + 1) * lanes)
                    logits = side[r, c] + product[r, c]
                    ids = at[3] + tile * lanes + lax.broadcasted_iota(jnp.int32, logits.shape, 1)
                    top, totals, target = fold(logits, ids, wanted[r], top, totals, target)
                new[0, r] = top
                new[1, r] = totals
                new[2, r] = target

            by_rows(rows, finish)

    if hear:

        @pl.when(jnp.logical_not(outer))
        def _():
            def add(r):
                if not end:
                    across[r] = side[r] + give[r]
                if start:
                    give[r] = middle[r] + product[r]

            by_rows(rows, add)


def step(model, s, where, features, head, side, middle, wanted, old, width):
    rows, depth = features.shape
    hear, start, end, last = s >= 0, 1 <= s <= steps, s >= steps, s >= 2
    whole = lambda shape: pl.BlockSpec(shape, lambda j, at: (0,) * len(shape))
    block = whole((rows, width))
    column = lambda k: pl.BlockSpec(
        (pl.Element(1), pl.Element(depth), pl.Element(width)),
        lambda j, at: (model, 0, pl.multiple_of(at[k] * lanes, lanes)),
    )
    flat = jax.ShapeDtypeStruct((rows, width), jnp.float32)
    return pl.pallas_call(
        functools.partial(step_kernel, start=start, hear=hear, end=end, last=last),
        grid_spec=pltpu.PrefetchScalarGridSpec(
            num_scalar_prefetch=1,
            grid=(1,),
            in_specs=[
                whole((rows, depth)),
                column(0),
                column(1),
                block,
                block,
                whole((rows, 1)),
                whole((3, rows, lanes)),
            ],
            out_specs=[block, block, whole((3, rows, lanes))],
            scratch_shapes=[pltpu.VMEM((rows, width), jnp.float32)],
        ),
        out_shape=[flat, flat, jax.ShapeDtypeStruct((3, rows, lanes), jnp.float32)],
        compiler_params=settings,
        cost_estimate=pl.CostEstimate(
            flops=4 * rows * depth * width, bytes_accessed=16 * rows * width, transcendentals=0
        ),
    )(where, features, head, head, side, middle, wanted, old)


def whole_kernel(at, *refs):
    count = (len(refs) - 3) // 3
    features, parts, wanted, out, logits = refs[:count], refs[count:-3], refs[-3], refs[-2], refs[-1]
    width = parts[0].shape[2]
    for half in range(2):

        def multiply(r):
            total = None
            for k in range(count):
                columns = parts[half * count + k][0]
                term = jnp.dot(features[k][0, r], columns, preferred_element_type=jnp.float32)
                total = term if total is None else total + term
            logits[r] = total

        def tiles(r):
            if half == 0:
                top = jnp.full((32, lanes), lowest, jnp.float32)
                totals, target = jnp.zeros_like(top), jnp.zeros_like(top)
            else:
                top, totals, target = out[0, 0, r], out[1, 0, r], out[2, 0, r]
            for tile in range(width // lanes):
                first = at[count] + half * width + tile * lanes
                values = logits[r, tile * lanes : (tile + 1) * lanes]
                ids = first + lax.broadcasted_iota(jnp.int32, values.shape, 1)
                top, totals, target = fold(values, ids, wanted[r], top, totals, target)
            out[0, 0, r] = top
            out[1, 0, r] = totals
            out[2, 0, r] = target

        by_rows(logits.shape[0], multiply, 128)
        by_rows(logits.shape[0], tiles)


def whole_statistics(features, early, late, targets, first):
    layer = lax.axis_index("dp")
    count = len(early)
    models, tokens, _ = features.shape
    depth, width = early[0].shape[1:]
    at = jnp.stack([layer ^ k for k in range(count)] + [first]).astype(jnp.int32)
    part = pl.BlockSpec((1, depth, width), lambda m, at: (m, 0, 0))
    return pl.pallas_call(
        whole_kernel,
        grid_spec=pltpu.PrefetchScalarGridSpec(
            num_scalar_prefetch=1,
            grid=(models,),
            in_specs=[
                pl.BlockSpec((1, tokens, depth), lambda m, at, k=k: (m, 0, at[k]))
                for k in range(count)
            ]
            + [part] * (2 * count)
            + [pl.BlockSpec((tokens, 1), lambda m, at: (0, 0))],
            out_specs=pl.BlockSpec((3, 1, tokens, lanes), lambda m, at: (0, m, 0, 0)),
            scratch_shapes=[pltpu.VMEM((tokens, width), jnp.float32)],
        ),
        out_shape=jax.ShapeDtypeStruct((3, models, tokens, lanes), jnp.float32),
        compiler_params=settings,
        cost_estimate=pl.CostEstimate(
            flops=4 * models * tokens * depth * count * width, bytes_accessed=8 << 20, transcendentals=0
        ),
    )(at, *([features] * count), *early, *late, targets[:, None])


def across_lanes(stats):
    peak = jnp.max(stats[0], axis=-1)
    totals = jnp.sum(stats[1] * jnp.exp(stats[0] - peak[..., None]), axis=-1)
    return peak, totals, jnp.sum(stats[2], axis=-1)


def chained(rows, everything, head, targets, lengths, vocab_first, near, far, early, late, part, first):
    layer = lax.axis_index("dp")
    models, depth = head.shape[:2]
    slot_count = everything.shape[1] // lengths.shape[0]
    outer = jnp.logical_or(layer == 0, layer == 3)
    ends = jnp.cumsum(lengths)
    starts = ends - lengths
    packed = jnp.arange(rows)
    rollout = jnp.sum(packed[:, None] >= ends[None, :], axis=1)
    offset = jnp.sum(
        jnp.where(rollout[:, None] == jnp.arange(lengths.shape[0])[None, :], starts[None, :], 0), axis=1
    )
    source = jnp.where(packed < ends[-1], rollout * slot_count + packed - offset, -1)
    picks = source[:, None] == jnp.arange(everything.shape[1])[None, :]
    wanted = jnp.sum(jnp.where(picks, targets[None, :], 0), axis=1)[:, None]
    features = lax.dynamic_slice_in_dim(everything, layer * depth, depth, 2)
    features = jnp.einsum(
        "kt,mtd->mkd", picks.astype(jnp.bfloat16), features, preferred_element_type=jnp.float32
    ).astype(jnp.bfloat16)
    features = [features[m] for m in range(models)]
    width = part // steps

    into, out = [(0, 1), (3, 2)], [(1, 0), (2, 3)]
    blank = jnp.zeros((rows, width), jnp.float32)
    side = [blank] * models
    middle = [blank] * models
    begin = jnp.concatenate(
        [jnp.full((1, rows, lanes), lowest, jnp.float32), jnp.zeros((2, rows, lanes), jnp.float32)]
    )
    found = [begin] * models
    aside = None
    for s in range(-1, steps + 2):
        far_at = jnp.where(outer, far + (s + 1) * width, far + s * width)
        near_at = jnp.where(outer, near + (s - 2) * width, near + (s - 1) * width)
        far_at = jnp.clip(far_at, 0, head.shape[2] - width)
        near_at = jnp.clip(near_at, 0, head.shape[2] - width)
        where = jnp.stack(
            [far_at // lanes, near_at // lanes, outer.astype(jnp.int32), vocab_first + near_at]
        ).astype(jnp.int32)
        for m in range(models):
            give, across, fresh = step(
                m, s, where, features[m], head, side[m], middle[m], wanted, found[m], width
            )
            if s >= 2:
                found[m] = fresh
            perm = (into if s + 1 < steps else []) + (out if 1 <= s <= steps else [])
            if perm:
                side[m] = lax.ppermute(give, "dp", perm)
            if 0 <= s < steps:
                middle[m] = lax.ppermute(across, "dp", [(1, 2), (2, 1)])
        if s == 2:
            everything, side = lax.optimization_barrier((everything, side))
            aside = whole_statistics(everything, early, late, targets, first)
    stats = jnp.stack(across_lanes(jnp.stack(found, axis=1)))
    floor = jnp.array([lowest, 0.0, 0.0], jnp.float32)[:, None, None]
    stats = jnp.where(outer, stats, floor)
    stats = jnp.pad(stats, ((0, 0), (0, 0), (0, slot_count)))
    stats = jnp.stack(
        [lax.dynamic_slice_in_dim(stats, starts[r], slot_count, 2) for r in range(lengths.shape[0])],
        axis=2,
    )
    aside = jnp.stack(across_lanes(aside)).reshape(stats.shape)
    return jnp.stack(both(stats, aside))


def body(
    pages,
    page_table,
    page_count,
    last_len,
    targets,
    mix_key,
    w_key,
    w_value,
    ln_gain,
    ln_bias,
    head,
):
    tensor_count = lax.axis_size("tensor")
    layer_count = lax.axis_size("dp")
    layer = lax.axis_index("dp")
    place = lax.axis_index("tensor")
    models, rows_held, page_len, width_local = pages.shape
    width = ln_gain.shape[1]
    page_cap = page_table.shape[1]
    slot_count = page_cap * page_len
    share = slot_count // tensor_count
    depth = head.shape[1]
    vocab_held = head.shape[2]
    vocab_part = vocab_held // layer_count

    states = None
    own_rows = page_table[layer]
    for k in range(layer_count):
        wanted = page_table[layer ^ k]
        block = jnp.take(pages, wanted % rows_held, axis=1)
        got = block if k == 0 else swap(block, "dp", k)
        here = (own_rows // rows_held) == (layer ^ k)
        here = jnp.logical_and(here, jnp.arange(page_cap) < page_count[layer])
        got = jnp.where(here[None, :, None, None], got, jnp.zeros_like(got))
        states = got if states is None else states + got

    lengths = (page_count - 1) * page_len + last_len
    wanted = jnp.concatenate(ordered(spread(targets, "dp"), layer), axis=0).reshape(-1)
    head, states, wanted = lax.optimization_barrier((head, states, wanted))

    chain = layer_count == 4
    whole = vocab_part // 4 if chain else vocab_part

    def columns(first, count):
        parts = []
        for k in range(layer_count):
            start = (layer ^ k) * whole + first
            part = plain(lax.dynamic_slice_in_dim(head, start, count, 2))
            parts.append(part if k == 0 else plain(swap(part, "dp", k)))
        return parts

    split = whole // 2
    early = columns(0, split)
    live = page_count[0] > 0
    tracks = routes(models)

    states = states.reshape(models, slot_count, width_local)
    state_f = states.astype(jnp.float32)
    previous = jnp.concatenate(
        [jnp.zeros((models, 1, width_local), jnp.float32), state_f[:, :-1]], axis=1
    )
    shifted = (state_f + (previous - state_f) * mix_key[:, None, :]).astype(jnp.bfloat16)

    def mix(shifted, state_f):
        mine = (jnp.arange(tensor_count) == place)[None, None, :, None]
        value = jnp.stack([gather_tensor(shifted[m], place, tracks[m]) for m in range(models)])
        value = value.transpose(0, 2, 1, 3).reshape(models, slot_count, width)
        hidden = jnp.einsum("msd,mdf->msf", value, w_key, preferred_element_type=jnp.float32)
        key_act = (jnp.maximum(hidden, 0.0) ** 2).astype(jnp.bfloat16)
        mixed = jnp.einsum("msf,mfd->msd", key_act, w_value, preferred_element_type=jnp.float32)
        mixed = mixed.reshape(models, slot_count, tensor_count, width_local)
        mixed = mixed + jnp.where(mine, state_f[:, :, None, :], 0.0)
        mixed = mixed.reshape(models, tensor_count, share, width)
        rows = []
        for m in range(models):
            residual = scatter_tensor(mixed[m], place, tracks[m])
            average = jnp.sum(residual, axis=-1) / width
            variance = jnp.sum(residual * residual, axis=-1) / width - average * average
            normed = (
                (residual - average[..., None]) * lax.rsqrt(variance + epsilon)[..., None]
            ) * ln_gain[m] + ln_bias[m]
            rows.append(normed.astype(jnp.bfloat16))
        return jnp.stack(rows)

    normed = section(live, mix, shifted, state_f)
    normed, early = lax.optimization_barrier((normed, early))
    layers = jnp.stack(ordered(spread(normed, "dp"), layer), axis=1)
    layers, head = lax.optimization_barrier((layers, head))
    late = columns(split, whole - split)

    def everywhere(column):
        values = []
        for m in range(models):
            value = gather_tensor(column[m], place, tracks[m]).transpose(1, 0, 2, 3)
            values.append(value.reshape(layer_count * slot_count, width))
        return jnp.stack(values)

    everything = section(live, everywhere, layers)

    def statistics(features, parts, first):
        logits = None
        for k in range(layer_count):
            rows = lax.dynamic_slice_in_dim(features, (layer ^ k) * depth, depth, 2)
            term = jnp.einsum("msd,mdv->msv", rows, parts[k], preferred_element_type=jnp.float32)
            logits = term if logits is None else logits + term
        start = place * vocab_held + layer * whole + first
        return reduced(logits, start, wanted)

    everything, early, late = lax.optimization_barrier((everything, early, late))
    if chain:
        part = (vocab_held - layer_count * whole) // 2
        low = layer < 2
        near = layer_count * whole + jnp.where(low, 0, part)
        far = layer_count * whole + jnp.where(low, part, 0)
        sizes = [224, 256, 288, 320, 352, 384, layer_count * slot_count]
        first = place * vocab_held + layer * whole
        branches = [functools.partial(chained, rows, part=part, first=first) for rows in sizes]
        bucket = sum((jnp.sum(lengths) > size).astype(jnp.int32) for size in sizes[:-1])
        stats = lax.switch(
            bucket,
            branches,
            everything,
            head,
            wanted,
            lengths,
            place * vocab_held,
            near,
            far,
            early,
            late,
        )
    else:
        stats = both(statistics(everything, early, 0), statistics(everything, late, split))
        stats = jnp.stack(stats).reshape(3, models, layer_count, slot_count)

    stats = stats.reshape(3, models, layer_count, slot_count)
    mine = []
    for k in range(layer_count):
        part = lax.dynamic_index_in_dim(stats, layer ^ k, 2, False)
        mine.append(part if k == 0 else swap(part, "dp", k))
    mine = jnp.concatenate(ordered(gather_chips(jnp.stack(ordered(mine, layer))), place))
    top = jnp.max(mine[:, 0], axis=0)
    totals = jnp.sum(mine[:, 1] * jnp.exp(mine[:, 0] - top), axis=0)
    logp = jnp.sum(mine[:, 2], axis=0) - top - jnp.log(totals)

    valid = jnp.arange(slot_count) < lengths[layer]
    policy_row = jnp.where(valid, logp[0], 0.0)
    ratio = jnp.sum(jnp.where(valid, logp[0] - logp[1], 0.0))
    token_part = lax.dynamic_slice_in_dim(policy_row, place * share, share)[None, :]
    return (token_part, ratio[None])


def solution(mesh):
    placed = (
        P(None, "dp", None, "tensor"),
        P(),
        P(),
        P(),
        P("dp", None),
        P(None, "tensor"),
        P(None, None, "tensor"),
        P(None, "tensor", None),
        P(),
        P(),
        P(None, "dp", "tensor"),
    )
    return jax.shard_map(
        body, mesh=mesh, in_specs=placed, out_specs=(P("dp", "tensor"), P("dp")), check_vma=False
    )
```

```python
import functools

import jax
import jax.numpy as jnp
from jax import lax
from jax.experimental import pallas as pl
from jax.experimental.pallas import tpu as pltpu
from jax.experimental.layout import Layout, with_layout_constraint
from jax.sharding import PartitionSpec as P

epsilon = 1e-05


def swap(value, axis, mask):
    count = lax.axis_size(axis)
    return lax.ppermute(value, axis, [(i, i ^ mask) for i in range(count)])


def ordered(pieces, index):
    pieces = list(pieces)
    bit = 1
    while bit < len(pieces):
        flip = (index & bit) != 0
        pieces = [jnp.where(flip, pieces[k ^ bit], pieces[k]) for k in range(len(pieces))]
        bit *= 2
    return pieces


def gather_chips(value):
    count = lax.axis_size("tensor")
    far = [value] + [swap(value, "tensor", k) for k in range(2, count, 2)]
    pieces = []
    for piece in far:
        pieces += [piece, swap(piece, "tensor", 1)]
    return pieces


def plain(value):
    return with_layout_constraint(value, Layout(major_to_minor=tuple(range(value.ndim))))


def spread(value, axis):
    return [value] + [swap(value, axis, k) for k in range(1, lax.axis_size(axis))]


def routes(models):
    bits = lax.axis_size("tensor").bit_length() - 1
    return [[1 + (b + m) % (bits - 1) for b in range(bits - 1)] for m in range(models)]


def gather_tensor(value, place, route):
    bits = route + [0]
    for bit in bits:
        other = swap(value, "tensor", 1 << bit)
        flip = ((place >> bit) & 1) != 0
        value = jnp.stack([jnp.where(flip, other, value), jnp.where(flip, value, other)])
    seen = bits[::-1]
    order = [seen.index(b) for b in sorted(bits, reverse=True)]
    rest = list(range(len(bits), value.ndim))
    value = value.transpose(order + rest)
    return value.reshape((1 << len(bits),) + value.shape[len(bits) :])


def scatter_tensor(value, place, route):
    count = value.shape[0]
    left = list(range(count.bit_length() - 2, -1, -1))
    value = value.reshape((2,) * len(left) + value.shape[1:])
    for bit in [0] + route:
        axis = left.index(bit)
        mine = (place >> bit) & 1
        keep = lax.dynamic_index_in_dim(value, mine, axis, False)
        give = lax.dynamic_index_in_dim(value, 1 - mine, axis, False)
        value = keep + swap(give, "tensor", 1 << bit)
        left.remove(bit)
    return value


def section(live, work, *operands):
    shapes = jax.eval_shape(work, *operands)
    idle = lambda *_: jax.tree.map(lambda s: jnp.zeros(s.shape, s.dtype), shapes)
    return lax.cond(live, work, idle, *operands)


def reduced(logits, first, wanted):
    matches = (jnp.arange(logits.shape[-1]) + first)[None, :] == wanted[:, None]
    peak = jnp.max(logits, axis=-1)
    totals = jnp.sum(jnp.exp(logits - peak[..., None]), axis=-1)
    return peak, totals, jnp.sum(jnp.where(matches, logits, 0.0), axis=-1)


def both(one, other):
    peak = jnp.maximum(one[0], other[0])
    totals = one[1] * jnp.exp(one[0] - peak) + other[1] * jnp.exp(other[0] - peak)
    return peak, totals, one[2] + other[2]


lowest = -3e38
steps = 8


lanes = 128
settings = pltpu.CompilerParams(vmem_limit_bytes=40 << 20)


def fold(logits, ids, wanted, peak, totals, target):
    top = jnp.maximum(peak, logits)
    totals = totals * jnp.exp(peak - top) + jnp.exp(logits - top)
    return top, totals, target + jnp.where(ids == wanted, logits, 0.0)


def by_rows(count, work, group=32):
    def one(i, _):
        work(pl.ds(pl.multiple_of(i * group, group), group))
        return 0

    lax.fori_loop(0, count // group, one, 0)


def step_kernel(
    at, features, far, near, side, middle, wanted, old, give, across, new, product, *, start, hear, end, last
):
    outer = at[2] != 0
    rows = features.shape[0]

    def multiply(r):
        value = features[r]
        if not end:
            give[r] = jnp.dot(value, far[0], preferred_element_type=jnp.float32)
        if start or last:
            product[r] = jnp.dot(value, near[0], preferred_element_type=jnp.float32)

    group = max(g for g in range(16, 113, 16) if rows % g == 0)
    by_rows(rows, multiply, group if group >= 64 else rows // 2)
    if last:

        @pl.when(outer)
        def _():
            def finish(r):
                top, totals, target = old[0, r], old[1, r], old[2, r]
                for tile in range(side.shape[1] // lanes):
                    c = slice(tile * lanes, (tile + 1) * lanes)
                    logits = side[r, c] + product[r, c]
                    ids = at[3] + tile * lanes + lax.broadcasted_iota(jnp.int32, logits.shape, 1)
                    top, totals, target = fold(logits, ids, wanted[r], top, totals, target)
                new[0, r] = top
                new[1, r] = totals
                new[2, r] = target

            by_rows(rows, finish)

    if hear:

        @pl.when(jnp.logical_not(outer))
        def _():
            def add(r):
                if not end:
                    across[r] = side[r] + give[r]
                if start:
                    give[r] = middle[r] + product[r]

            by_rows(rows, add)


def step(model, s, where, features, head, side, middle, wanted, old, width):
    rows, depth = features.shape
    hear, start, end, last = s >= 0, 1 <= s <= steps, s >= steps, s >= 2
    whole = lambda shape: pl.BlockSpec(shape, lambda j, at: (0,) * len(shape))
    block = whole((rows, width))
    column = lambda k: pl.BlockSpec(
        (pl.Element(1), pl.Element(depth), pl.Element(width)),
        lambda j, at: (model, 0, pl.multiple_of(at[k] * lanes, lanes)),
    )
    flat = jax.ShapeDtypeStruct((rows, width), jnp.float32)
    return pl.pallas_call(
        functools.partial(step_kernel, start=start, hear=hear, end=end, last=last),
        grid_spec=pltpu.PrefetchScalarGridSpec(
            num_scalar_prefetch=1,
            grid=(1,),
            in_specs=[
                whole((rows, depth)),
                column(0),
                column(1),
                block,
                block,
                whole((rows, 1)),
                whole((3, rows, lanes)),
            ],
            out_specs=[block, block, whole((3, rows, lanes))],
            scratch_shapes=[pltpu.VMEM((rows, width), jnp.float32)],
        ),
        out_shape=[flat, flat, jax.ShapeDtypeStruct((3, rows, lanes), jnp.float32)],
        compiler_params=settings,
        cost_estimate=pl.CostEstimate(
            flops=4 * rows * depth * width, bytes_accessed=16 * rows * width, transcendentals=0
        ),
    )(where, features, head, head, side, middle, wanted, old)


def whole_kernel(at, *refs):
    count = (len(refs) - 3) // 3
    features, parts, wanted, out, logits = refs[:count], refs[count:-3], refs[-3], refs[-2], refs[-1]
    width = parts[0].shape[2]
    for half in range(2):

        def multiply(r):
            total = None
            for k in range(count):
                columns = parts[half * count + k][0]
                term = jnp.dot(features[k][0, r], columns, preferred_element_type=jnp.float32)
                total = term if total is None else total + term
            logits[r] = total

        def tiles(r):
            if half == 0:
                top = jnp.full((32, lanes), lowest, jnp.float32)
                totals, target = jnp.zeros_like(top), jnp.zeros_like(top)
            else:
                top, totals, target = out[0, 0, r], out[1, 0, r], out[2, 0, r]
            for tile in range(width // lanes):
                first = at[count] + half * width + tile * lanes
                values = logits[r, tile * lanes : (tile + 1) * lanes]
                ids = first + lax.broadcasted_iota(jnp.int32, values.shape, 1)
                top, totals, target = fold(values, ids, wanted[r], top, totals, target)
            out[0, 0, r] = top
            out[1, 0, r] = totals
            out[2, 0, r] = target

        by_rows(logits.shape[0], multiply, 128)
        by_rows(logits.shape[0], tiles)


def whole_statistics(features, early, late, targets, first):
    layer = lax.axis_index("dp")
    count = len(early)
    models, tokens, _ = features.shape
    depth, width = early[0].shape[1:]
    at = jnp.stack([layer ^ k for k in range(count)] + [first]).astype(jnp.int32)
    part = pl.BlockSpec((1, depth, width), lambda m, at: (m, 0, 0))
    return pl.pallas_call(
        whole_kernel,
        grid_spec=pltpu.PrefetchScalarGridSpec(
            num_scalar_prefetch=1,
            grid=(models,),
            in_specs=[
                pl.BlockSpec((1, tokens, depth), lambda m, at, k=k: (m, 0, at[k]))
                for k in range(count)
            ]
            + [part] * (2 * count)
            + [pl.BlockSpec((tokens, 1), lambda m, at: (0, 0))],
            out_specs=pl.BlockSpec((3, 1, tokens, lanes), lambda m, at: (0, m, 0, 0)),
            scratch_shapes=[pltpu.VMEM((tokens, width), jnp.float32)],
        ),
        out_shape=jax.ShapeDtypeStruct((3, models, tokens, lanes), jnp.float32),
        compiler_params=settings,
        cost_estimate=pl.CostEstimate(
            flops=4 * models * tokens * depth * count * width, bytes_accessed=8 << 20, transcendentals=0
        ),
    )(at, *([features] * count), *early, *late, targets[:, None])


def across_lanes(stats):
    peak = jnp.max(stats[0], axis=-1)
    totals = jnp.sum(stats[1] * jnp.exp(stats[0] - peak[..., None]), axis=-1)
    return peak, totals, jnp.sum(stats[2], axis=-1)


def chained(rows, everything, head, targets, lengths, vocab_first, near, far, early, late, part, first):
    layer = lax.axis_index("dp")
    models, depth = head.shape[:2]
    slot_count = everything.shape[1] // lengths.shape[0]
    outer = jnp.logical_or(layer == 0, layer == 3)
    ends = jnp.cumsum(lengths)
    starts = ends - lengths
    packed = jnp.arange(rows)
    rollout = jnp.sum(packed[:, None] >= ends[None, :], axis=1)
    offset = jnp.sum(
        jnp.where(rollout[:, None] == jnp.arange(lengths.shape[0])[None, :], starts[None, :], 0), axis=1
    )
    source = jnp.where(packed < ends[-1], rollout * slot_count + packed - offset, -1)
    picks = source[:, None] == jnp.arange(everything.shape[1])[None, :]
    wanted = jnp.sum(jnp.where(picks, targets[None, :], 0), axis=1)[:, None]
    features = lax.dynamic_slice_in_dim(everything, layer * depth, depth, 2)
    features = jnp.einsum(
        "kt,mtd->mkd", picks.astype(jnp.bfloat16), features, preferred_element_type=jnp.float32
    ).astype(jnp.bfloat16)
    features = [features[m] for m in range(models)]
    width = part // steps

    into, out = [(0, 1), (3, 2)], [(1, 0), (2, 3)]
    blank = jnp.zeros((rows, width), jnp.float32)
    side = [blank] * models
    middle = [blank] * models
    begin = jnp.concatenate(
        [jnp.full((1, rows, lanes), lowest, jnp.float32), jnp.zeros((2, rows, lanes), jnp.float32)]
    )
    found = [begin] * models
    aside = None
    for s in range(-1, steps + 2):
        far_at = jnp.where(outer, far + (s + 1) * width, far + s * width)
        near_at = jnp.where(outer, near + (s - 2) * width, near + (s - 1) * width)
        far_at = jnp.clip(far_at, 0, head.shape[2] - width)
        near_at = jnp.clip(near_at, 0, head.shape[2] - width)
        where = jnp.stack(
            [far_at // lanes, near_at // lanes, outer.astype(jnp.int32), vocab_first + near_at]
        ).astype(jnp.int32)
        for m in range(models):
            give, across, fresh = step(
                m, s, where, features[m], head, side[m], middle[m], wanted, found[m], width
            )
            if s >= 2:
                found[m] = fresh
            perm = (into if s + 1 < steps else []) + (out if 1 <= s <= steps else [])
            if perm:
                side[m] = lax.ppermute(give, "dp", perm)
            if 0 <= s < steps:
                middle[m] = lax.ppermute(across, "dp", [(1, 2), (2, 1)])
        if s == 2:
            everything, side = lax.optimization_barrier((everything, side))
            aside = whole_statistics(everything, early, late, targets, first)
    stats = jnp.stack(across_lanes(jnp.stack(found, axis=1)))
    floor = jnp.array([lowest, 0.0, 0.0], jnp.float32)[:, None, None]
    stats = jnp.where(outer, stats, floor)
    stats = jnp.pad(stats, ((0, 0), (0, 0), (0, slot_count)))
    stats = jnp.stack(
        [lax.dynamic_slice_in_dim(stats, starts[r], slot_count, 2) for r in range(lengths.shape[0])],
        axis=2,
    )
    aside = jnp.stack(across_lanes(aside)).reshape(stats.shape)
    return jnp.stack(both(stats, aside))


def direct(everything, head, targets, lengths, vocab_first, near, far, early, late, first):
    layer = lax.axis_index("dp")
    layer_count = len(early)
    models = head.shape[0]
    begin = layer_count * early[0].shape[2] * 2
    rest = (head.shape[2] - begin) // layer_count
    width = rest // 4
    total = None
    for group in range(3):
        if group == 0:
            halves, start = [early, late], first
        else:
            halves = []
            for half in range(2):
                shift = ((group - 1) * 2 + half) * width
                parts = []
                for k in range(layer_count):
                    at = begin + (layer ^ k) * rest + shift
                    part = plain(lax.dynamic_slice_in_dim(head, at, width, 2))
                    parts.append(part if k == 0 else plain(swap(part, "dp", k)))
                halves.append(parts)
            start = vocab_first + begin + layer * rest + (group - 1) * 2 * width
        found = across_lanes(whole_statistics(everything, *halves, targets, start))
        total = found if total is None else both(total, found)
    return jnp.stack(total).reshape(3, models, lengths.shape[0], -1)


def body(
    pages,
    page_table,
    page_count,
    last_len,
    targets,
    mix_key,
    w_key,
    w_value,
    ln_gain,
    ln_bias,
    head,
):
    tensor_count = lax.axis_size("tensor")
    layer_count = lax.axis_size("dp")
    layer = lax.axis_index("dp")
    place = lax.axis_index("tensor")
    models, rows_held, page_len, width_local = pages.shape
    width = ln_gain.shape[1]
    page_cap = page_table.shape[1]
    slot_count = page_cap * page_len
    share = slot_count // tensor_count
    depth = head.shape[1]
    vocab_held = head.shape[2]
    vocab_part = vocab_held // layer_count

    states = None
    own_rows = page_table[layer]
    for k in range(layer_count):
        wanted = page_table[layer ^ k]
        block = jnp.take(pages, wanted % rows_held, axis=1)
        got = block if k == 0 else swap(block, "dp", k)
        here = (own_rows // rows_held) == (layer ^ k)
        here = jnp.logical_and(here, jnp.arange(page_cap) < page_count[layer])
        got = jnp.where(here[None, :, None, None], got, jnp.zeros_like(got))
        states = got if states is None else states + got

    lengths = (page_count - 1) * page_len + last_len
    wanted = jnp.concatenate(ordered(spread(targets, "dp"), layer), axis=0).reshape(-1)
    head, states, wanted = lax.optimization_barrier((head, states, wanted))

    chain = layer_count == 4
    whole = vocab_part // 4 if chain else vocab_part

    def columns(first, count):
        parts = []
        for k in range(layer_count):
            start = (layer ^ k) * whole + first
            part = plain(lax.dynamic_slice_in_dim(head, start, count, 2))
            parts.append(part if k == 0 else plain(swap(part, "dp", k)))
        return parts

    split = whole // 2
    early = columns(0, split)
    live = page_count[0] > 0
    tracks = routes(models)

    states = states.reshape(models, slot_count, width_local)
    state_f = states.astype(jnp.float32)
    previous = jnp.concatenate(
        [jnp.zeros((models, 1, width_local), jnp.float32), state_f[:, :-1]], axis=1
    )
    shifted = (state_f + (previous - state_f) * mix_key[:, None, :]).astype(jnp.bfloat16)

    def mix(shifted, state_f):
        mine = (jnp.arange(tensor_count) == place)[None, None, :, None]
        value = jnp.stack([gather_tensor(shifted[m], place, tracks[m]) for m in range(models)])
        value = value.transpose(0, 2, 1, 3).reshape(models, slot_count, width)
        hidden = jnp.einsum("msd,mdf->msf", value, w_key, preferred_element_type=jnp.float32)
        key_act = (jnp.maximum(hidden, 0.0) ** 2).astype(jnp.bfloat16)
        mixed = jnp.einsum("msf,mfd->msd", key_act, w_value, preferred_element_type=jnp.float32)
        mixed = mixed.reshape(models, slot_count, tensor_count, width_local)
        mixed = mixed + jnp.where(mine, state_f[:, :, None, :], 0.0)
        mixed = mixed.reshape(models, tensor_count, share, width)
        rows = []
        for m in range(models):
            residual = scatter_tensor(mixed[m], place, tracks[m])
            average = jnp.sum(residual, axis=-1) / width
            variance = jnp.sum(residual * residual, axis=-1) / width - average * average
            normed = (
                (residual - average[..., None]) * lax.rsqrt(variance + epsilon)[..., None]
            ) * ln_gain[m] + ln_bias[m]
            rows.append(normed.astype(jnp.bfloat16))
        return jnp.stack(rows)

    normed = section(live, mix, shifted, state_f)
    normed, early = lax.optimization_barrier((normed, early))
    layers = jnp.stack(ordered(spread(normed, "dp"), layer), axis=1)
    layers, head = lax.optimization_barrier((layers, head))
    late = columns(split, whole - split)

    def everywhere(column):
        values = []
        for m in range(models):
            value = gather_tensor(column[m], place, tracks[m]).transpose(1, 0, 2, 3)
            values.append(value.reshape(layer_count * slot_count, width))
        return jnp.stack(values)

    everything = section(live, everywhere, layers)

    def statistics(features, parts, first):
        logits = None
        for k in range(layer_count):
            rows = lax.dynamic_slice_in_dim(features, (layer ^ k) * depth, depth, 2)
            term = jnp.einsum("msd,mdv->msv", rows, parts[k], preferred_element_type=jnp.float32)
            logits = term if logits is None else logits + term
        start = place * vocab_held + layer * whole + first
        return reduced(logits, start, wanted)

    everything, early, late = lax.optimization_barrier((everything, early, late))
    if chain:
        part = (vocab_held - layer_count * whole) // 2
        low = layer < 2
        near = layer_count * whole + jnp.where(low, 0, part)
        far = layer_count * whole + jnp.where(low, part, 0)
        sizes = [224, 256, 288, 320, 352]
        first = place * vocab_held + layer * whole
        branches = [functools.partial(chained, rows, part=part, first=first) for rows in sizes]
        branches.append(functools.partial(direct, first=first))
        bucket = sum((jnp.sum(lengths) > size).astype(jnp.int32) for size in sizes)
        stats = lax.switch(
            bucket,
            branches,
            everything,
            head,
            wanted,
            lengths,
            place * vocab_held,
            near,
            far,
            early,
            late,
        )
    else:
        stats = both(statistics(everything, early, 0), statistics(everything, late, split))
        stats = jnp.stack(stats).reshape(3, models, layer_count, slot_count)

    stats = stats.reshape(3, models, layer_count, slot_count)
    mine = []
    for k in range(layer_count):
        part = lax.dynamic_index_in_dim(stats, layer ^ k, 2, False)
        mine.append(part if k == 0 else swap(part, "dp", k))
    mine = jnp.concatenate(ordered(gather_chips(jnp.stack(ordered(mine, layer))), place))
    top = jnp.max(mine[:, 0], axis=0)
    totals = jnp.sum(mine[:, 1] * jnp.exp(mine[:, 0] - top), axis=0)
    logp = jnp.sum(mine[:, 2], axis=0) - top - jnp.log(totals)

    valid = jnp.arange(slot_count) < lengths[layer]
    policy_row = jnp.where(valid, logp[0], 0.0)
    ratio = jnp.sum(jnp.where(valid, logp[0] - logp[1], 0.0))
    token_part = lax.dynamic_slice_in_dim(policy_row, place * share, share)[None, :]
    return (token_part, ratio[None])


def solution(mesh):
    placed = (
        P(None, "dp", None, "tensor"),
        P(),
        P(),
        P(),
        P("dp", None),
        P(None, "tensor"),
        P(None, None, "tensor"),
        P(None, "tensor", None),
        P(),
        P(),
        P(None, "dp", "tensor"),
    )
    return jax.shard_map(
        body, mesh=mesh, in_specs=placed, out_specs=(P("dp", "tensor"), P("dp")), check_vma=False
    )
```

```python
import functools

import jax
import jax.numpy as jnp
from jax import lax
from jax.experimental import pallas as pl
from jax.experimental.pallas import tpu as pltpu
from jax.experimental.layout import Layout, with_layout_constraint
from jax.sharding import PartitionSpec as P

epsilon = 1e-05


def swap(value, axis, mask):
    count = lax.axis_size(axis)
    return lax.ppermute(value, axis, [(i, i ^ mask) for i in range(count)])


def ordered(pieces, index):
    pieces = list(pieces)
    bit = 1
    while bit < len(pieces):
        flip = (index & bit) != 0
        pieces = [jnp.where(flip, pieces[k ^ bit], pieces[k]) for k in range(len(pieces))]
        bit *= 2
    return pieces


def gather_chips(value):
    count = lax.axis_size("tensor")
    far = [value] + [swap(value, "tensor", k) for k in range(2, count, 2)]
    pieces = []
    for piece in far:
        pieces += [piece, swap(piece, "tensor", 1)]
    return pieces


def plain(value):
    return with_layout_constraint(value, Layout(major_to_minor=tuple(range(value.ndim))))


def spread(value, axis):
    return [value] + [swap(value, axis, k) for k in range(1, lax.axis_size(axis))]


def routes(models):
    bits = lax.axis_size("tensor").bit_length() - 1
    return [[1 + (b + m) % (bits - 1) for b in range(bits - 1)] for m in range(models)]


def gather_tensor(value, place, route):
    bits = route + [0]
    for bit in bits:
        other = swap(value, "tensor", 1 << bit)
        flip = ((place >> bit) & 1) != 0
        value = jnp.stack([jnp.where(flip, other, value), jnp.where(flip, value, other)])
    seen = bits[::-1]
    order = [seen.index(b) for b in sorted(bits, reverse=True)]
    rest = list(range(len(bits), value.ndim))
    value = value.transpose(order + rest)
    return value.reshape((1 << len(bits),) + value.shape[len(bits) :])


def scatter_tensor(value, place, route):
    count = value.shape[0]
    left = list(range(count.bit_length() - 2, -1, -1))
    value = value.reshape((2,) * len(left) + value.shape[1:])
    for bit in [0] + route:
        axis = left.index(bit)
        mine = (place >> bit) & 1
        keep = lax.dynamic_index_in_dim(value, mine, axis, False)
        give = lax.dynamic_index_in_dim(value, 1 - mine, axis, False)
        value = keep + swap(give, "tensor", 1 << bit)
        left.remove(bit)
    return value


def section(live, work, *operands):
    shapes = jax.eval_shape(work, *operands)
    idle = lambda *_: jax.tree.map(lambda s: jnp.zeros(s.shape, s.dtype), shapes)
    return lax.cond(live, work, idle, *operands)


def reduced(logits, first, wanted):
    matches = (jnp.arange(logits.shape[-1]) + first)[None, :] == wanted[:, None]
    peak = jnp.max(logits, axis=-1)
    totals = jnp.sum(jnp.exp(logits - peak[..., None]), axis=-1)
    return peak, totals, jnp.sum(jnp.where(matches, logits, 0.0), axis=-1)


def both(one, other):
    peak = jnp.maximum(one[0], other[0])
    totals = one[1] * jnp.exp(one[0] - peak) + other[1] * jnp.exp(other[0] - peak)
    return peak, totals, one[2] + other[2]


lowest = -3e38
steps = 8


lanes = 128
settings = pltpu.CompilerParams(vmem_limit_bytes=40 << 20)


def fold(logits, ids, wanted, peak, totals, target):
    top = jnp.maximum(peak, logits)
    totals = totals * jnp.exp(peak - top) + jnp.exp(logits - top)
    return top, totals, target + jnp.where(ids == wanted, logits, 0.0)


def by_rows(count, work, group=32):
    def one(i, _):
        work(pl.ds(pl.multiple_of(i * group, group), group))
        return 0

    lax.fori_loop(0, count // group, one, 0)


def step_kernel(
    at, features, far, near, side, middle, wanted, old, give, across, new, product, *, start, hear, end, last
):
    outer = at[2] != 0
    rows = features.shape[0]

    def multiply(r):
        value = features[r]
        if not end:
            give[r] = jnp.dot(value, far[0], preferred_element_type=jnp.float32)
        if start or last:
            product[r] = jnp.dot(value, near[0], preferred_element_type=jnp.float32)

    group = max(g for g in range(16, 113, 16) if rows % g == 0)
    by_rows(rows, multiply, group if group >= 64 else rows // 2)
    if last:

        @pl.when(outer)
        def _():
            def finish(r):
                top, totals, target = old[0, r], old[1, r], old[2, r]
                for tile in range(side.shape[1] // lanes):
                    c = slice(tile * lanes, (tile + 1) * lanes)
                    logits = side[r, c] + product[r, c]
                    ids = at[3] + tile * lanes + lax.broadcasted_iota(jnp.int32, logits.shape, 1)
                    top, totals, target = fold(logits, ids, wanted[r], top, totals, target)
                new[0, r] = top
                new[1, r] = totals
                new[2, r] = target

            by_rows(rows, finish)

    if hear:

        @pl.when(jnp.logical_not(outer))
        def _():
            def add(r):
                if not end:
                    across[r] = side[r] + give[r]
                if start:
                    give[r] = middle[r] + product[r]

            by_rows(rows, add)


def step(model, s, where, features, head, side, middle, wanted, old, width):
    rows, depth = features.shape
    hear, start, end, last = s >= 0, 1 <= s <= steps, s >= steps, s >= 2
    whole = lambda shape: pl.BlockSpec(shape, lambda j, at: (0,) * len(shape))
    block = whole((rows, width))
    column = lambda k: pl.BlockSpec(
        (pl.Element(1), pl.Element(depth), pl.Element(width)),
        lambda j, at: (model, 0, pl.multiple_of(at[k] * lanes, lanes)),
    )
    flat = jax.ShapeDtypeStruct((rows, width), jnp.float32)
    return pl.pallas_call(
        functools.partial(step_kernel, start=start, hear=hear, end=end, last=last),
        grid_spec=pltpu.PrefetchScalarGridSpec(
            num_scalar_prefetch=1,
            grid=(1,),
            in_specs=[
                whole((rows, depth)),
                column(0),
                column(1),
                block,
                block,
                whole((rows, 1)),
                whole((3, rows, lanes)),
            ],
            out_specs=[block, block, whole((3, rows, lanes))],
            scratch_shapes=[pltpu.VMEM((rows, width), jnp.float32)],
        ),
        out_shape=[flat, flat, jax.ShapeDtypeStruct((3, rows, lanes), jnp.float32)],
        compiler_params=settings,
        cost_estimate=pl.CostEstimate(
            flops=4 * rows * depth * width, bytes_accessed=16 * rows * width, transcendentals=0
        ),
    )(where, features, head, head, side, middle, wanted, old)


def whole_kernel(at, *refs):
    count = (len(refs) - 3) // 3
    features, parts, wanted, out, logits = refs[:count], refs[count:-3], refs[-3], refs[-2], refs[-1]
    width = parts[0].shape[2]
    for half in range(2):

        def multiply(r):
            total = None
            for k in range(count):
                columns = parts[half * count + k][0]
                term = jnp.dot(features[k][0, r], columns, preferred_element_type=jnp.float32)
                total = term if total is None else total + term
            logits[r] = total

        def tiles(r):
            if half == 0:
                top = jnp.full((32, lanes), lowest, jnp.float32)
                totals, target = jnp.zeros_like(top), jnp.zeros_like(top)
            else:
                top, totals, target = out[0, 0, r], out[1, 0, r], out[2, 0, r]
            for tile in range(width // lanes):
                first = at[count] + half * width + tile * lanes
                values = logits[r, tile * lanes : (tile + 1) * lanes]
                ids = first + lax.broadcasted_iota(jnp.int32, values.shape, 1)
                top, totals, target = fold(values, ids, wanted[r], top, totals, target)
            out[0, 0, r] = top
            out[1, 0, r] = totals
            out[2, 0, r] = target

        by_rows(logits.shape[0], multiply, 128)
        by_rows(logits.shape[0], tiles)


def whole_statistics(features, early, late, targets, first, base=0, models=2):
    layer = lax.axis_index("dp")
    count = len(early)
    tokens = features.shape[1]
    depth, width = early[0].shape[1:]
    at = jnp.stack([layer ^ k for k in range(count)] + [first]).astype(jnp.int32)
    part = pl.BlockSpec((1, depth, width), lambda m, at: (base + m, 0, 0))
    return pl.pallas_call(
        whole_kernel,
        grid_spec=pltpu.PrefetchScalarGridSpec(
            num_scalar_prefetch=1,
            grid=(models,),
            in_specs=[
                pl.BlockSpec((1, tokens, depth), lambda m, at, k=k: (base + m, 0, at[k]))
                for k in range(count)
            ]
            + [part] * (2 * count)
            + [pl.BlockSpec((tokens, 1), lambda m, at: (0, 0))],
            out_specs=pl.BlockSpec((3, 1, tokens, lanes), lambda m, at: (0, m, 0, 0)),
            scratch_shapes=[pltpu.VMEM((tokens, width), jnp.float32)],
        ),
        out_shape=jax.ShapeDtypeStruct((3, models, tokens, lanes), jnp.float32),
        compiler_params=settings,
        cost_estimate=pl.CostEstimate(
            flops=4 * models * tokens * depth * count * width, bytes_accessed=8 << 20, transcendentals=0
        ),
    )(at, *([features] * count), *early, *late, targets[:, None])


def across_lanes(stats):
    peak = jnp.max(stats[0], axis=-1)
    totals = jnp.sum(stats[1] * jnp.exp(stats[0] - peak[..., None]), axis=-1)
    return peak, totals, jnp.sum(stats[2], axis=-1)


def chained(rows, everything, head, targets, lengths, vocab_first, near, far, early, late, part, first):
    layer = lax.axis_index("dp")
    models, depth = head.shape[:2]
    slot_count = everything.shape[1] // lengths.shape[0]
    outer = jnp.logical_or(layer == 0, layer == 3)
    ends = jnp.cumsum(lengths)
    starts = ends - lengths
    packed = jnp.arange(rows)
    rollout = jnp.sum(packed[:, None] >= ends[None, :], axis=1)
    offset = jnp.sum(
        jnp.where(rollout[:, None] == jnp.arange(lengths.shape[0])[None, :], starts[None, :], 0), axis=1
    )
    source = jnp.where(packed < ends[-1], rollout * slot_count + packed - offset, -1)
    picks = source[:, None] == jnp.arange(everything.shape[1])[None, :]
    wanted = jnp.sum(jnp.where(picks, targets[None, :], 0), axis=1)[:, None]
    features = lax.dynamic_slice_in_dim(everything, layer * depth, depth, 2)
    features = jnp.einsum(
        "kt,mtd->mkd", picks.astype(jnp.bfloat16), features, preferred_element_type=jnp.float32
    ).astype(jnp.bfloat16)
    features = [features[m] for m in range(models)]
    width = part // steps

    into, out = [(0, 1), (3, 2)], [(1, 0), (2, 3)]
    blank = jnp.zeros((rows, width), jnp.float32)
    side = [blank] * models
    middle = [blank] * models
    begin = jnp.concatenate(
        [jnp.full((1, rows, lanes), lowest, jnp.float32), jnp.zeros((2, rows, lanes), jnp.float32)]
    )
    found = [begin] * models
    aside = []
    for s in range(-1, steps + 2):
        far_at = jnp.where(outer, far + (s + 1) * width, far + s * width)
        near_at = jnp.where(outer, near + (s - 2) * width, near + (s - 1) * width)
        far_at = jnp.clip(far_at, 0, head.shape[2] - width)
        near_at = jnp.clip(near_at, 0, head.shape[2] - width)
        where = jnp.stack(
            [far_at // lanes, near_at // lanes, outer.astype(jnp.int32), vocab_first + near_at]
        ).astype(jnp.int32)
        for m in range(models):
            give, across, fresh = step(
                m, s, where, features[m], head, side[m], middle[m], wanted, found[m], width
            )
            if s >= 2:
                found[m] = fresh
            perm = (into if s + 1 < steps else []) + (out if 1 <= s <= steps else [])
            if perm:
                side[m] = lax.ppermute(give, "dp", perm)
            if 0 <= s < steps:
                middle[m] = lax.ppermute(across, "dp", [(1, 2), (2, 1)])
        if s in (2, 4):
            everything, side[0] = lax.optimization_barrier((everything, side[0]))
            aside.append(whole_statistics(everything, early, late, targets, first, len(aside), 1))
        if s in (3, 5):
            aside[-1], side[1] = lax.optimization_barrier((aside[-1], side[1]))
    stats = jnp.stack(across_lanes(jnp.stack(found, axis=1)))
    floor = jnp.array([lowest, 0.0, 0.0], jnp.float32)[:, None, None]
    stats = jnp.where(outer, stats, floor)
    stats = jnp.pad(stats, ((0, 0), (0, 0), (0, slot_count)))
    stats = jnp.stack(
        [lax.dynamic_slice_in_dim(stats, starts[r], slot_count, 2) for r in range(lengths.shape[0])],
        axis=2,
    )
    aside = jnp.stack(across_lanes(jnp.concatenate(aside, axis=1))).reshape(stats.shape)
    return jnp.stack(both(stats, aside))


def direct(everything, head, targets, lengths, vocab_first, near, far, early, late, first):
    layer = lax.axis_index("dp")
    layer_count = len(early)
    models = head.shape[0]
    begin = layer_count * early[0].shape[2] * 2
    rest = (head.shape[2] - begin) // layer_count
    width = rest // 4
    total = None
    for group in range(3):
        if group == 0:
            halves, start = [early, late], first
        else:
            halves = []
            for half in range(2):
                shift = ((group - 1) * 2 + half) * width
                parts = []
                for k in range(layer_count):
                    at = begin + (layer ^ k) * rest + shift
                    part = plain(lax.dynamic_slice_in_dim(head, at, width, 2))
                    parts.append(part if k == 0 else plain(swap(part, "dp", k)))
                halves.append(parts)
            start = vocab_first + begin + layer * rest + (group - 1) * 2 * width
        found = across_lanes(whole_statistics(everything, *halves, targets, start))
        total = found if total is None else both(total, found)
    return jnp.stack(total).reshape(3, models, lengths.shape[0], -1)


def body(
    pages,
    page_table,
    page_count,
    last_len,
    targets,
    mix_key,
    w_key,
    w_value,
    ln_gain,
    ln_bias,
    head,
):
    tensor_count = lax.axis_size("tensor")
    layer_count = lax.axis_size("dp")
    layer = lax.axis_index("dp")
    place = lax.axis_index("tensor")
    models, rows_held, page_len, width_local = pages.shape
    width = ln_gain.shape[1]
    page_cap = page_table.shape[1]
    slot_count = page_cap * page_len
    share = slot_count // tensor_count
    depth = head.shape[1]
    vocab_held = head.shape[2]
    vocab_part = vocab_held // layer_count

    states = None
    own_rows = page_table[layer]
    for k in range(layer_count):
        wanted = page_table[layer ^ k]
        block = jnp.take(pages, wanted % rows_held, axis=1)
        got = block if k == 0 else swap(block, "dp", k)
        here = (own_rows // rows_held) == (layer ^ k)
        here = jnp.logical_and(here, jnp.arange(page_cap) < page_count[layer])
        got = jnp.where(here[None, :, None, None], got, jnp.zeros_like(got))
        states = got if states is None else states + got

    lengths = (page_count - 1) * page_len + last_len
    wanted = jnp.concatenate(ordered(spread(targets, "dp"), layer), axis=0).reshape(-1)
    head, states, wanted = lax.optimization_barrier((head, states, wanted))

    chain = layer_count == 4
    whole = vocab_part // 4 if chain else vocab_part

    def columns(first, count):
        parts = []
        for k in range(layer_count):
            start = (layer ^ k) * whole + first
            part = plain(lax.dynamic_slice_in_dim(head, start, count, 2))
            parts.append(part if k == 0 else plain(swap(part, "dp", k)))
        return parts

    split = whole // 2
    early = columns(0, split)
    live = page_count[0] > 0
    tracks = routes(models)

    states = states.reshape(models, slot_count, width_local)
    state_f = states.astype(jnp.float32)
    previous = jnp.concatenate(
        [jnp.zeros((models, 1, width_local), jnp.float32), state_f[:, :-1]], axis=1
    )
    shifted = (state_f + (previous - state_f) * mix_key[:, None, :]).astype(jnp.bfloat16)

    def mix(shifted, state_f):
        mine = (jnp.arange(tensor_count) == place)[None, None, :, None]
        value = jnp.stack([gather_tensor(shifted[m], place, tracks[m]) for m in range(models)])
        value = value.transpose(0, 2, 1, 3).reshape(models, slot_count, width)
        hidden = jnp.einsum("msd,mdf->msf", value, w_key, preferred_element_type=jnp.float32)
        key_act = (jnp.maximum(hidden, 0.0) ** 2).astype(jnp.bfloat16)
        mixed = jnp.einsum("msf,mfd->msd", key_act, w_value, preferred_element_type=jnp.float32)
        mixed = mixed.reshape(models, slot_count, tensor_count, width_local)
        mixed = mixed + jnp.where(mine, state_f[:, :, None, :], 0.0)
        mixed = mixed.reshape(models, tensor_count, share, width)
        rows = []
        for m in range(models):
            residual = scatter_tensor(mixed[m], place, tracks[m])
            average = jnp.sum(residual, axis=-1) / width
            variance = jnp.sum(residual * residual, axis=-1) / width - average * average
            normed = (
                (residual - average[..., None]) * lax.rsqrt(variance + epsilon)[..., None]
            ) * ln_gain[m] + ln_bias[m]
            rows.append(normed.astype(jnp.bfloat16))
        return jnp.stack(rows)

    normed = section(live, mix, shifted, state_f)
    normed, early = lax.optimization_barrier((normed, early))
    layers = jnp.stack(ordered(spread(normed, "dp"), layer), axis=1)
    layers, head = lax.optimization_barrier((layers, head))
    late = columns(split, whole - split)

    def everywhere(column):
        values = []
        for m in range(models):
            value = gather_tensor(column[m], place, tracks[m]).transpose(1, 0, 2, 3)
            values.append(value.reshape(layer_count * slot_count, width))
        return jnp.stack(values)

    everything = section(live, everywhere, layers)

    def statistics(features, parts, first):
        logits = None
        for k in range(layer_count):
            rows = lax.dynamic_slice_in_dim(features, (layer ^ k) * depth, depth, 2)
            term = jnp.einsum("msd,mdv->msv", rows, parts[k], preferred_element_type=jnp.float32)
            logits = term if logits is None else logits + term
        start = place * vocab_held + layer * whole + first
        return reduced(logits, start, wanted)

    everything, early, late = lax.optimization_barrier((everything, early, late))
    if chain:
        part = (vocab_held - layer_count * whole) // 2
        low = layer < 2
        near = layer_count * whole + jnp.where(low, 0, part)
        far = layer_count * whole + jnp.where(low, part, 0)
        sizes = [224, 256, 288, 320, 352]
        first = place * vocab_held + layer * whole
        branches = [functools.partial(chained, rows, part=part, first=first) for rows in sizes]
        branches.append(functools.partial(direct, first=first))
        bucket = sum((jnp.sum(lengths) > size).astype(jnp.int32) for size in sizes)
        stats = lax.switch(
            bucket,
            branches,
            everything,
            head,
            wanted,
            lengths,
            place * vocab_held,
            near,
            far,
            early,
            late,
        )
    else:
        stats = both(statistics(everything, early, 0), statistics(everything, late, split))
        stats = jnp.stack(stats).reshape(3, models, layer_count, slot_count)

    stats = stats.reshape(3, models, layer_count, slot_count)
    mine = []
    for k in range(layer_count):
        part = lax.dynamic_index_in_dim(stats, layer ^ k, 2, False)
        mine.append(part if k == 0 else swap(part, "dp", k))
    mine = jnp.concatenate(ordered(gather_chips(jnp.stack(ordered(mine, layer))), place))
    top = jnp.max(mine[:, 0], axis=0)
    totals = jnp.sum(mine[:, 1] * jnp.exp(mine[:, 0] - top), axis=0)
    logp = jnp.sum(mine[:, 2], axis=0) - top - jnp.log(totals)

    valid = jnp.arange(slot_count) < lengths[layer]
    policy_row = jnp.where(valid, logp[0], 0.0)
    ratio = jnp.sum(jnp.where(valid, logp[0] - logp[1], 0.0))
    token_part = lax.dynamic_slice_in_dim(policy_row, place * share, share)[None, :]
    return (token_part, ratio[None])


def solution(mesh):
    placed = (
        P(None, "dp", None, "tensor"),
        P(),
        P(),
        P(),
        P("dp", None),
        P(None, "tensor"),
        P(None, None, "tensor"),
        P(None, "tensor", None),
        P(),
        P(),
        P(None, "dp", "tensor"),
    )
    return jax.shard_map(
        body, mesh=mesh, in_specs=placed, out_specs=(P("dp", "tensor"), P("dp")), check_vma=False
    )
```
